32 devices in a mesh: seq: 16 (over z, y, core), tp: 2 (over x).
Axes of the slice: x: 2, y: 2, z: 4, core: 2. Of those that a mesh axis runs over, the one named last changes fastest.
Arguments:
- hidden: bfloat16 [4096, 4096], P('seq', 'tp'), may hold values from -6 to 6
- neighbours: bfloat16 [64, 256, 896], P('seq'), may hold values from -6 to 6
- enc_gain: float32 [896], replicated, may hold values from 0.25 to 1.75
- enc_w1: bfloat16 [896, 3584], P(None, 'tp'), may hold values from -0.1875 to 0.1875
- enc_w2: bfloat16 [3584, 896], P('tp'), may hold values from -0.09375 to 0.09375
- key_weight: bfloat16 [896, 4096], P(None, 'tp'), may hold values from -0.1875 to 0.1875
- value_weight: bfloat16 [896, 4096], P(None, 'tp'), may hold values from -0.1875 to 0.1875
- dec_gain: float32 [4096], replicated, may hold values from 0.25 to 1.75
- query_weight: bfloat16 [4096, 4096], P('seq', 'tp'), may hold values from -0.09375 to 0.09375
- out_weight: bfloat16 [4096, 4096], P('tp', 'seq'), may hold values from -0.09375 to 0.09375
Outputs:
- mixed: bfloat16 [4096, 4096], P('seq', 'tp')
The draws below stay inside these ranges and needn't reach their ends.
All inputs are finite; a program needn't handle non-finite values.
Results may differ from the reference program's by a relative error of at most 0.015.
Values may be sent and summed in bfloat16 or wider, within the bound.
No kernel may reach another device: no remote copies, remote signals or barrier semaphores. Data moves between devices by JAX's collectives and lax.ppermute only.
A program may use at most 128 MiB of HBM per device.

```python
import jax
import jax.numpy as jnp
from jax import lax

D = 4096
HEADS = 32
HD = 128
E = 896
EFF = 3584
M = 64
NEIGH = 2
RLEN = 128
TOKENS = 4096
SPANS = 64
N_TP = 2


def shard_levels(key, shape, cuts, low, high):
    def one(axis_at, shards_of):
        steps = jax.random.uniform(jax.random.fold_in(jax.random.fold_in(key, 6), axis_at), (shards_of,), jnp.float32, low / len(cuts), high / len(cuts))
        return jnp.repeat(jnp.exp(steps), shape[axis_at] // shards_of).reshape((-1,) + (1,) * (len(shape) - axis_at - 1))

    factor_of = one(*cuts[0])
    for cut in cuts[1:]:
        factor_of = factor_of * one(*cut)
    return factor_of


def normal_values(rng, extent, deviation, limit, pieces=(), held_as=jnp.bfloat16):
    result = deviation * jax.random.normal(rng, extent, jnp.float32)
    if pieces:
        result = result * shard_levels(rng, extent, pieces, -0.22, 0.18)
    return jnp.clip(result, -limit, limit).astype(held_as)


def setup_inputs(seed: int = 0) -> dict:
    streams_of = jax.random.split(jax.random.key(seed), 11)
    return {
        "hidden": normal_values(streams_of[0], (TOKENS, D), 1.0, 6.0, ((0, 16), (1, 2))),
        "neighbours": normal_values(streams_of[1], (SPANS, NEIGH * RLEN, E), 1.0, 6.0, ((0, 16),)),
        "enc_gain": jnp.clip(1.0 + 0.15 * jax.random.normal(streams_of[2], (E,), jnp.float32), 0.25, 1.75),
        "enc_w1": normal_values(streams_of[3], (E, EFF), E ** -0.5, 0.1875, ((1, 2),)),
        "enc_w2": normal_values(streams_of[4], (EFF, E), EFF ** -0.5, 0.09375, ((0, 2),)),
        "key_weight": normal_values(streams_of[5], (E, HEADS * HD), E ** -0.5, 0.1875, ((1, 2),)),
        "value_weight": normal_values(streams_of[6], (E, HEADS * HD), E ** -0.5, 0.1875, ((1, 2),)),
        "dec_gain": jnp.clip(1.0 + 0.15 * jax.random.normal(streams_of[7], (D,), jnp.float32), 0.25, 1.75),
        "query_weight": normal_values(streams_of[8], (D, HEADS * HD), D ** -0.5, 0.09375, ((0, 16), (1, 2))),
        "out_weight": normal_values(streams_of[9], (HEADS * HD, D), (HEADS * HD) ** -0.5, 0.09375, ((0, 2), (1, 16))),
    }


def rms_scale(values32, gain):
    return values32 * lax.rsqrt(lax.optimization_barrier(jnp.mean(values32 * values32, axis=-1, keepdims=True)) + 1e-06) * gain.astype(jnp.float32)

def reference(hidden, neighbours, enc_gain, enc_w1, enc_w2, key_weight, value_weight, dec_gain, query_weight, out_weight):
    hidden32 = hidden.astype(jnp.float32)
    dec_norm = rms_scale(hidden32, dec_gain).astype(jnp.bfloat16)
    query = jnp.dot(dec_norm, query_weight, preferred_element_type=jnp.float32).astype(jnp.bfloat16)
    flat = neighbours.reshape(SPANS * NEIGH * RLEN, E)
    enc_norm = rms_scale(flat.astype(jnp.float32), enc_gain).astype(jnp.bfloat16)
    inner = jax.nn.relu(jnp.dot(enc_norm, enc_w1, preferred_element_type=jnp.float32)).astype(jnp.bfloat16)
    encoded = (flat.astype(jnp.float32) + jnp.dot(inner, enc_w2, preferred_element_type=jnp.float32)).astype(jnp.bfloat16)
    keys = jnp.dot(encoded, key_weight, preferred_element_type=jnp.float32).astype(jnp.bfloat16)
    values = jnp.dot(encoded, value_weight, preferred_element_type=jnp.float32).astype(jnp.bfloat16)
    keys = keys.reshape(SPANS, NEIGH * RLEN, HEADS, HD)
    values = values.reshape(SPANS, NEIGH * RLEN, HEADS, HD)
    blank = jnp.zeros((1, NEIGH * RLEN, HEADS, HD), jnp.bfloat16)
    keys = jnp.concatenate([blank, keys], axis=0)
    values = jnp.concatenate([blank, values], axis=0)
    grouped = jnp.pad(query, ((1, M - 1), (0, 0))).reshape(SPANS + 1, M, HEADS, HD)
    scores = jnp.einsum('cmhd,cnhd->chmn', grouped.astype(jnp.float32), keys.astype(jnp.float32)) * HD ** (-0.5)
    probs = jax.nn.softmax(scores, axis=-1).astype(jnp.bfloat16)
    attn = jnp.einsum('chmn,cnhd->cmhd', probs.astype(jnp.float32), values.astype(jnp.float32)).astype(jnp.bfloat16)
    attn = attn.reshape((SPANS + 1) * M, HEADS * HD)[1:TOKENS + 1]
    position = jnp.arange(TOKENS, dtype=jnp.int32)[:, None]
    attn = jnp.where(position >= M - 1, attn, jnp.zeros_like(attn))
    group_width = HEADS * HD // N_TP
    branch = jnp.zeros((TOKENS, D), jnp.float32)
    for group in range(N_TP):
        lower = group * group_width
        partial_value = jnp.dot(attn[:, lower:lower + group_width], out_weight[lower:lower + group_width], preferred_element_type=jnp.float32).astype(jnp.bfloat16)
        partial_value = lax.optimization_barrier(partial_value)
        branch = branch + partial_value.astype(jnp.float32)
    return (hidden32 + branch).astype(jnp.bfloat16)
```

```python
import functools

import jax
import jax.numpy as jnp
from jax import lax
from jax.experimental import pallas as pl
from jax.experimental.pallas import tpu as pltpu
from jax.sharding import PartitionSpec as P

HD = 128
M = 64
KEYS = 256


def factors(count):
    core = 2 if count % 2 == 0 else 1
    y = 2 if (count // core) % 2 == 0 else 1
    return count // (core * y), y, core


def swap(value, axis, stride, size):
    count = lax.axis_size(axis)
    if size == 1:
        return value
    pairs = [(i, i + stride if (i // stride) % 2 == 0 else i - stride) for i in range(count)]
    return lax.ppermute(value, axis, pairs)


def ring(value, axis, stride):
    count = lax.axis_size(axis)
    return lax.ppermute(value, axis, [(i, (i + stride) % count) for i in range(count)])


def gather_blocks(block, last_by_ring):
    depth, y, core = factors(lax.axis_size("seq"))
    own, other = [block], []
    for k in range(depth):
        last = k == depth - 1
        if y == 2:
            if last and last_by_ring and depth > 1:
                other.append(ring(other[-1], "seq", core * y))
            else:
                other.append(swap(own[k], "seq", core, y))
        if not last:
            own.append(ring(own[k], "seq", core * y))
    return [[own[k]] + ([other[k]] if y == 2 else []) for k in range(depth)]


def rms_scale(values32, gain):
    return (
        values32 * lax.rsqrt(jnp.mean(values32 * values32, axis=-1, keepdims=True) + 1e-06) * gain
    )


def feed_partial(tokens, enc_gain, first_weight, second_weight):
    enc_norm = rms_scale(tokens.astype(jnp.float32), enc_gain).astype(jnp.bfloat16)
    inner = jax.nn.relu(jnp.dot(enc_norm, first_weight, preferred_element_type=jnp.float32)).astype(
        jnp.bfloat16
    )
    return jnp.dot(inner, second_weight, preferred_element_type=jnp.float32).astype(jnp.bfloat16)


def tp_sum(value):
    if lax.axis_size("tp") == 2:
        return value.astype(jnp.float32) + swap(value, "tp", 1, 2).astype(jnp.float32)
    return lax.psum(value, "tp").astype(jnp.float32)


def ordered(flag, first, second, axis):
    return jnp.concatenate(
        [jnp.where(flag, first, second), jnp.where(flag, second, first)], axis=axis
    )


def attend_kernel(heads, spans, q_ref, k_ref, v_ref, o_ref):
    for h in range(heads):
        cols = slice(h * HD, (h + 1) * HD)
        for s in range(spans):
            rows = slice(s * M, (s + 1) * M)
            keys = slice(s * KEYS, (s + 1) * KEYS)
            scores = lax.dot_general(
                q_ref[rows, cols],
                k_ref[keys, cols],
                (((1,), (1,)), ((), ())),
                preferred_element_type=jnp.float32,
            ) * HD ** (-0.5)
            shifted = jnp.exp(scores - jnp.max(scores, axis=-1, keepdims=True))
            probs = (shifted / jnp.sum(shifted, axis=-1, keepdims=True)).astype(jnp.bfloat16)
            o_ref[rows, cols] = jnp.dot(
                probs, v_ref[keys, cols], preferred_element_type=jnp.float32
            ).astype(jnp.bfloat16)


def attend(query, keys, values):
    rows, width = query.shape
    spans = rows // M
    heads = 2 if (width // HD) % 2 == 0 else 1
    block = heads * HD
    return pl.pallas_call(
        functools.partial(attend_kernel, heads, spans),
        grid=(width // block,),
        in_specs=[
            pl.BlockSpec((rows, block), lambda i: (0, i)),
            pl.BlockSpec((spans * KEYS, block), lambda i: (0, i)),
            pl.BlockSpec((spans * KEYS, block), lambda i: (0, i)),
        ],
        out_specs=pl.BlockSpec((rows, block), lambda i: (0, i)),
        out_shape=jax.ShapeDtypeStruct((rows, width), jnp.bfloat16),
        compiler_params=pltpu.CompilerParams(vmem_limit_bytes=24 * 1024 * 1024),
        cost_estimate=pl.CostEstimate(
            flops=4 * rows * KEYS * width,
            bytes_accessed=4 * (rows + spans * KEYS) * width,
            transcendentals=rows * KEYS * width // HD,
        ),
        name="attend",
    )(query, keys, values)


def per_device(
    hidden,
    neighbours,
    enc_gain,
    enc_w1,
    enc_w2,
    key_weight,
    value_weight,
    dec_gain,
    query_weight,
    out_weight,
):
    tok_rows, feat = hidden.shape
    span_count, key_rows, width = neighbours.shape
    n_seq, n_tp = lax.axis_size("seq"), lax.axis_size("tp")
    depth, n_y, n_core = factors(n_seq)
    me = lax.axis_index("seq")
    tp_at = lax.axis_index("tp")
    core_at, y_at, z_at = me % n_core, (me // n_core) % n_y, me // (n_core * n_y)
    core_first, y_first = core_at == 0, y_at == 0

    q_rows, q_cols = query_weight.shape
    per_core = q_cols // n_core
    streams = 2
    q_width = per_core // streams
    q_blocks = []
    for h in range(streams):
        mine = lax.dynamic_slice(query_weight, (0, core_at * per_core + h * q_width), (q_rows, q_width))
        if n_core == 2:
            theirs = lax.dynamic_slice(
                query_weight, (0, (1 - core_at) * per_core + h * q_width), (q_rows, q_width)
            )
            mine = ordered(core_first, mine, swap(theirs, "seq", 1, 2), 0)
        q_blocks.append(gather_blocks(mine, h == 0))

    if n_tp == 2:
        features = ordered(tp_at == 0, hidden, swap(hidden, "tp", 1, 2), 1)
    else:
        features = lax.all_gather(hidden, "tp", axis=1, tiled=True)
    dec_norm = rms_scale(features.astype(jnp.float32), dec_gain).astype(jnp.bfloat16)
    if n_core == 2:
        dec_norm = jnp.concatenate([dec_norm, swap(dec_norm, "seq", 1, 2)], axis=0)

    flat = neighbours.reshape(span_count * key_rows, width)
    pieces = 2
    piece_rows = flat.shape[0] // pieces
    encoded = []
    for i in range(pieces):
        part = flat[i * piece_rows : (i + 1) * piece_rows]
        summed = tp_sum(feed_partial(part, enc_gain, enc_w1, enc_w2))
        encoded.append((part.astype(jnp.float32) + summed).astype(jnp.bfloat16))
    earlier = lax.ppermute(
        encoded[-1][piece_rows - key_rows :], "seq", [(i, i + 1) for i in range(n_seq - 1)]
    )
    encoded = jnp.concatenate([earlier] + encoded, axis=0)
    keys = jnp.dot(encoded, key_weight, preferred_element_type=jnp.float32).astype(jnp.bfloat16)
    values = jnp.dot(encoded, value_weight, preferred_element_type=jnp.float32).astype(jnp.bfloat16)

    group = q_rows * n_core
    parts = []
    for h in range(streams):
        total = jnp.zeros((dec_norm.shape[0], q_width), jnp.float32)
        for k in range(depth):
            for j in range(n_y):
                at = ((z_at - k) % depth) * n_y + (y_at + j) % n_y
                total = total + jnp.dot(
                    lax.dynamic_slice(dec_norm, (0, at * group), (dec_norm.shape[0], group)),
                    q_blocks[h][k][j],
                    preferred_element_type=jnp.float32,
                )
        parts.append(total.astype(jnp.bfloat16))
    query = jnp.concatenate(parts, axis=1)
    if n_core == 2:
        query = ordered(core_first, query[:tok_rows], swap(query[tok_rows:], "seq", 1, 2), 1)

    grouped = jnp.pad(query, ((1, M - 1), (0, 0)))
    attn = attend(grouped, keys, values)[1 : tok_rows + 1]
    position = me * tok_rows + jnp.arange(tok_rows, dtype=jnp.int32)[:, None]
    attn = jnp.where(position >= M - 1, attn, jnp.zeros_like(attn))
    if n_core == 2:
        attn = jnp.concatenate([attn, swap(attn, "seq", 1, 2)], axis=0)

    o_rows, o_cols = out_weight.shape
    half = o_rows // streams
    o_blocks = [
        gather_blocks(out_weight[h * half : (h + 1) * half], h == 0) for h in range(streams)
    ]
    products = []
    for k in range(depth):
        made = []
        for j in range(n_y):
            total = sum(
                jnp.dot(
                    attn[:, h * half : (h + 1) * half],
                    o_blocks[h][k][j],
                    preferred_element_type=jnp.float32,
                )
                for h in range(streams)
            )
            made.append(total.astype(jnp.bfloat16))
        if n_core == 2:
            here = [m[:tok_rows] for m in made]
            there = swap(jnp.concatenate([m[tok_rows:] for m in made], axis=1), "seq", 1, 2)
            there = [there[:, j * o_cols : (j + 1) * o_cols] for j in range(n_y)]
            made = [ordered(core_first, a, b, 1) for a, b in zip(here, there)]
        products.append(ordered(y_first, made[0], made[1], 1) if n_y == 2 else made[0])

    if n_tp == 2 and depth % 4 == 0:
        pairs = depth // 2
        kept = []
        for p in range(pairs):
            mine = ((z_at - p) % depth) // pairs == tp_at
            sent = jnp.where(mine, products[p + pairs], products[p])
            stay = jnp.where(mine, products[p], products[p + pairs])
            kept.append(stay.astype(jnp.float32) + swap(sent, "tp", 1, 2).astype(jnp.float32))
        stacked = jnp.stack(kept, axis=0)
        order = (z_at - jnp.arange(pairs)) % pairs
        branch = jnp.take(stacked, order, axis=0)
        branch = jnp.moveaxis(branch, 0, 1).reshape(tok_rows, feat)
    else:
        stacked = jnp.stack(products, axis=0)
        order = (z_at - jnp.arange(depth)) % depth
        whole = jnp.moveaxis(jnp.take(stacked, order, axis=0), 0, 1).reshape(tok_rows, feat * n_tp)
        branch = lax.psum_scatter(whole, "tp", scatter_dimension=1, tiled=True).astype(jnp.float32)
    return (hidden.astype(jnp.float32) + branch).astype(jnp.bfloat16)


def solution(mesh):
    placed = (
        P("seq", "tp"),
        P("seq", None, None),
        P(),
        P(None, "tp"),
        P("tp", None),
        P(None, "tp"),
        P(None, "tp"),
        P(),
        P("seq", "tp"),
        P("tp", "seq"),
    )
    return jax.shard_map(
        per_device, mesh=mesh, in_specs=placed, out_specs=P("seq", "tp"), check_vma=False
    )
```

```python
import functools

import jax
import jax.numpy as jnp
from jax import lax
from jax.experimental import pallas as pl
from jax.experimental.pallas import tpu as pltpu
from jax.sharding import PartitionSpec as P

HD = 128
M = 64
KEYS = 256


def factors(count):
    core = 2 if count % 2 == 0 else 1
    y = 2 if (count // core) % 2 == 0 else 1
    return count // (core * y), y, core


def swap(value, axis, stride):
    count = lax.axis_size(axis)
    pairs = [(i, i + stride if (i // stride) % 2 == 0 else i - stride) for i in range(count)]
    return lax.ppermute(value, axis, pairs)


def ring(value, axis, stride):
    count = lax.axis_size(axis)
    return lax.ppermute(value, axis, [(i, (i + stride) % count) for i in range(count)])


def named(name):
    def wrap(function):
        def inner(*args):
            with jax.named_scope(name):
                return function(*args)

        return inner

    return wrap


def after(value, *done):
    return lax.optimization_barrier((value,) + done)[0]


class Stream:
    def __init__(self, name, block):
        self.depth, self.n_y, self.n_core = factors(lax.axis_size("seq"))
        self.name, self.blocks = name, {(0, 0): block}

    def fetch(self, k, j, way, mark):
        step = self.n_core * self.n_y
        with jax.named_scope(f"{self.name}_{k}_{j}"):
            if way == "y":
                made = swap(after(self.blocks[k, 0], *mark), "seq", self.n_core)
            elif way == "on":
                made = ring(after(self.blocks[k - 1, j], *mark), "seq", step)
            else:
                made = ring(after(self.blocks[(k + 1) % self.depth, j], *mark), "seq", -step)
        self.blocks[k, j] = made


def ordered(flag, first, second, axis):
    return jnp.concatenate(
        [jnp.where(flag, first, second), jnp.where(flag, second, first)], axis=axis
    )


WHOLE = pl.BlockSpec(memory_space=pltpu.VMEM)
SCALARS = pl.BlockSpec(memory_space=pltpu.SMEM)


def cost(flops, moved):
    return pl.CostEstimate(flops=int(flops), bytes_accessed=int(moved), transcendentals=0)


def params(mib):
    return pltpu.CompilerParams(vmem_limit_bytes=mib * 1024 * 1024)


def tiles(size, tile=256):
    return tile if size % tile == 0 else size


def encode_kernel(x_ref, gain_ref, first_ref, second_ref, out_ref, norm_ref, inner_ref):
    x = x_ref[...].astype(jnp.float32)
    scale = lax.rsqrt(jnp.mean(x * x, axis=-1, keepdims=True) + 1e-06)
    norm_ref[...] = (x * scale * gain_ref[...]).astype(jnp.bfloat16)
    units = first_ref.shape[1]
    tile = tiles(units)
    for n in range(0, units, tile):
        made = jnp.dot(norm_ref[...], first_ref[:, n : n + tile], preferred_element_type=jnp.float32)
        inner_ref[:, n : n + tile] = jnp.maximum(made, 0.0).astype(jnp.bfloat16)
    rows = tiles(x_ref.shape[0])
    for m in range(0, x_ref.shape[0], rows):
        out_ref[m : m + rows, :] = jnp.dot(
            inner_ref[m : m + rows, :], second_ref[...], preferred_element_type=jnp.float32
        ).astype(jnp.bfloat16)


def encode_partial(tokens, gain, first_weight, second_weight):
    rows = tokens.shape[0]
    return pl.pallas_call(
        encode_kernel,
        in_specs=[WHOLE] * 4,
        out_specs=WHOLE,
        out_shape=jax.ShapeDtypeStruct((rows, second_weight.shape[1]), jnp.bfloat16),
        scratch_shapes=[
            pltpu.VMEM(tokens.shape, jnp.bfloat16),
            pltpu.VMEM((rows, first_weight.shape[1]), jnp.bfloat16),
        ],
        compiler_params=params(14),
        cost_estimate=cost(4 * rows * tokens.shape[1] * first_weight.shape[1], 4 * first_weight.size),
        name="encode",
    )(tokens, gain, first_weight, second_weight)


def project_kernel(terms, *refs):
    part_refs, (k_in, v_in, enc_ref, k_ref, v_ref) = refs[:terms], refs[terms:]
    total = part_refs[0][...].astype(jnp.float32)
    if terms > 1:
        summed = part_refs[1][...].astype(jnp.float32)
        for ref in part_refs[2:]:
            summed = summed + ref[...].astype(jnp.float32)
        total = total + summed
    enc_ref[...] = total.astype(jnp.bfloat16)
    cols = k_in.shape[1]
    tile = tiles(cols)
    for w_ref, o_ref in ((k_in, k_ref), (v_in, v_ref)):
        for n in range(0, cols, tile):
            o_ref[:, n : n + tile] = jnp.dot(
                enc_ref[...], w_ref[:, n : n + tile], preferred_element_type=jnp.float32
            ).astype(jnp.bfloat16)


def project(parts, key_weight, value_weight):
    rows, width = parts[0].shape
    cols = key_weight.shape[1]
    return pl.pallas_call(
        functools.partial(project_kernel, len(parts)),
        in_specs=[WHOLE] * (len(parts) + 2),
        out_specs=[WHOLE] * 3,
        out_shape=[
            jax.ShapeDtypeStruct((rows, width), jnp.bfloat16),
            jax.ShapeDtypeStruct((rows, cols), jnp.bfloat16),
            jax.ShapeDtypeStruct((rows, cols), jnp.bfloat16),
        ],
        compiler_params=params(18),
        cost_estimate=cost(4 * rows * width * cols, 4 * key_weight.size),
        name="project",
    )(*parts, key_weight, value_weight)


def decode_kernel(at_ref, own_ref, came_ref, gain_ref, out_ref):
    own, came = own_ref[...].astype(jnp.float32), came_ref[...].astype(jnp.float32)
    shards, _, width = out_ref.shape
    half = shards // 2
    total = jnp.sum(own * own, axis=-1, keepdims=True) + jnp.sum(came * came, axis=-1, keepdims=True)
    scale = lax.rsqrt(total / (shards * width) + 1e-06)
    for i, ref in enumerate((own_ref, came_ref)):
        for g in range(half):
            to = at_ref[i] + g
            value = ref[:, g * width : (g + 1) * width].astype(jnp.float32)
            out_ref[to] = (value * scale * gain_ref[to]).astype(jnp.bfloat16)


def decode_norm(own_first, own, came, gain, shards):
    rows, half = own.shape
    width = 2 * half // shards
    at = jnp.where(own_first, jnp.array([0, shards // 2]), jnp.array([shards // 2, 0]))
    return pl.pallas_call(
        decode_kernel,
        in_specs=[SCALARS] + [WHOLE] * 3,
        out_specs=WHOLE,
        out_shape=jax.ShapeDtypeStruct((shards, rows, width), jnp.bfloat16),
        compiler_params=params(8),
        cost_estimate=cost(0, 10 * own.size),
        name="decode",
    )(at.astype(jnp.int32), own, came, gain.reshape(shards, 1, width))


def query_kernel(norms, blocks, more, at_ref, *refs):
    norm_refs, block_refs = refs[:norms], refs[norms : norms + blocks]
    out_ref = refs[-1]
    rows, depth = norm_refs[0].shape[1:]
    tile = tiles(out_ref.shape[1])
    for i, norm_ref in enumerate(norm_refs):
        own = slice(i * rows, (i + 1) * rows)
        for n in range(0, out_ref.shape[1], tile):
            cols = slice(n, n + tile)
            total, at = None, 0
            for block_ref in block_refs:
                for first in range(0, block_ref.shape[0], depth):
                    term = jnp.dot(
                        norm_ref[at_ref[at]],
                        block_ref[first : first + depth, cols],
                        preferred_element_type=jnp.float32,
                    )
                    total, at = term if total is None else total + term, at + 1
            if more:
                total = total + refs[-2][own, cols]
            out_ref[own, cols] = total.astype(out_ref.dtype)


def add_query(at, norms, blocks, total, dtype):
    more = () if total is None else (total,)
    shape = (len(norms) * norms[0].shape[1], blocks[0].shape[1])
    moved = sum(b.size for b in blocks)
    return pl.pallas_call(
        functools.partial(query_kernel, len(norms), len(blocks), len(more)),
        in_specs=[SCALARS] + [WHOLE] * (len(norms) + len(blocks) + len(more)),
        out_specs=WHOLE,
        out_shape=jax.ShapeDtypeStruct(shape, dtype),
        compiler_params=params(18),
        cost_estimate=cost(2 * shape[0] * moved, 2 * moved),
        name="query",
    )(at, *norms, *blocks, *more)


def out_kernel(attns, sizes, near_ref, *refs):
    attn_refs, block_refs, out_refs = refs[:attns], refs[attns:-attns], refs[-attns:]
    first = 0
    for i, counts in enumerate(sizes):
        for branch, count in enumerate(counts):
            parts = block_refs[first : first + count]
            first += count

            @pl.when(near_ref[i] == 1 - branch)
            def _(i=i, parts=parts):
                for attn_ref, out_ref in zip(attn_refs, out_refs):
                    total, row = None, 0
                    for ref in parts:
                        size = ref.shape[0]
                        term = jnp.dot(
                            attn_ref[:, row : row + size],
                            ref[...],
                            preferred_element_type=jnp.float32,
                        )
                        total, row = term if total is None else total + term, row + size
                    out_ref[i] = total.astype(jnp.bfloat16)


def out_products(near, attns, pairs):
    shape = jax.ShapeDtypeStruct(
        (len(pairs), attns[0].shape[0], pairs[0][0][0].shape[1]), jnp.bfloat16
    )
    flat = [part for pair in pairs for block in pair for part in block]
    return pl.pallas_call(
        functools.partial(out_kernel, len(attns), [[len(b) for b in pair] for pair in pairs]),
        in_specs=[SCALARS] + [WHOLE] * (len(attns) + len(flat)),
        out_specs=[WHOLE] * len(attns),
        out_shape=[shape] * len(attns),
        compiler_params=params(14),
        cost_estimate=cost(0, 1024),
        name="out",
    )(near, *attns, *flat)


def attend_kernel(heads, pieces, q_ref, *refs):
    k_refs, v_refs, o_ref = refs[: len(pieces)], refs[len(pieces) : -1], refs[-1]
    scale = HD ** (-0.5)
    units = [(p, s) for p, count in enumerate(pieces) for s in range(count)]
    for h in range(heads):
        cols = slice(h * HD, (h + 1) * HD)
        scores = []
        for u, (p, s) in enumerate(units):
            scores.append(
                lax.dot_general(
                    q_ref[u * M : (u + 1) * M, cols],
                    k_refs[p][s * KEYS : (s + 1) * KEYS, cols],
                    (((1,), (1,)), ((), ())),
                    preferred_element_type=jnp.float32,
                )
            )
        tops = [jnp.max(s, axis=-1, keepdims=True) for s in scores]
        exps = [jnp.exp((s - t) * scale) for s, t in zip(scores, tops)]
        scales = [1.0 / jnp.sum(e, axis=-1, keepdims=True) for e in exps]
        probs = [(e * r).astype(jnp.bfloat16) for e, r in zip(exps, scales)]
        for u, (p, s) in enumerate(units):
            o_ref[u * M : (u + 1) * M, cols] = jnp.dot(
                probs[u],
                v_refs[p][s * KEYS : (s + 1) * KEYS, cols],
                preferred_element_type=jnp.float32,
            ).astype(jnp.bfloat16)


def attend(query, keys, values):
    rows, width = query.shape
    heads = 2 if (width // HD) % 2 == 0 else 1
    block = heads * HD
    pieces = tuple(k.shape[0] // KEYS for k in keys)
    held = [pl.BlockSpec((k.shape[0], block), lambda i: (0, i)) for k in keys]
    return pl.pallas_call(
        functools.partial(attend_kernel, heads, pieces),
        grid=(width // block,),
        in_specs=[pl.BlockSpec((rows, block), lambda i: (0, i))] + held + held,
        out_specs=pl.BlockSpec((rows, block), lambda i: (0, i)),
        out_shape=jax.ShapeDtypeStruct((rows, width), jnp.bfloat16),
        compiler_params=params(10),
        cost_estimate=cost(0, 1024),
        name="attend",
    )(query, *keys, *values)


def per_device(
    hidden,
    neighbours,
    enc_gain,
    enc_w1,
    enc_w2,
    key_weight,
    value_weight,
    dec_gain,
    query_weight,
    out_weight,
):
    tok_rows, feat = hidden.shape
    span_count, key_rows, width = neighbours.shape
    n_seq, n_tp = lax.axis_size("seq"), lax.axis_size("tp")
    depth, n_y, n_core = factors(n_seq)
    me = lax.axis_index("seq")
    tp_at = lax.axis_index("tp")
    core_at, y_at, z_at = me % n_core, (me // n_core) % n_y, me // (n_core * n_y)
    core_first = core_at == 0

    q_rows, q_cols = query_weight.shape
    per_core = q_cols // n_core
    block = lax.dynamic_slice(query_weight, (0, core_at * per_core), (q_rows, per_core))
    if n_core == 2:
        theirs = lax.dynamic_slice(query_weight, (0, (1 - core_at) * per_core), (q_rows, per_core))
        block = jnp.concatenate([block, swap(theirs, "seq", 1)], axis=0)
    q_stream = Stream("query", block)

    o_rows, o_cols = out_weight.shape
    o_stream = Stream("out", out_weight)

    if n_tp == 2:
        hidden_came = swap(hidden, "tp", 1)
    else:
        hidden_came = lax.all_gather(hidden, "tp", axis=1, tiled=True)

    flat = neighbours.reshape(span_count * key_rows, width)
    piece_rows = flat.shape[0] // 2
    parts = [flat[i * piece_rows : (i + 1) * piece_rows] for i in range(2)]
    gain = enc_gain.reshape(1, width)
    v = {}

    @named("encode")
    def encode(i, mark):
        v["part", i] = encode_partial(after(parts[i], *mark), gain, enc_w1, enc_w2)
        return (v["part", i],)

    @named("encode_sum")
    def encode_sum(i, mark):
        own = after(v["part", i], *mark)
        if n_tp == 2:
            v["sum", i] = (own, swap(own, "tp", 1))
        else:
            v["sum", i] = (lax.psum(own, "tp"),)
        return v["sum", i]

    @named("decode")
    def decode(mark):
        came = after(hidden_came, *mark)
        if n_tp == 2:
            norm = decode_norm(tp_at == 0, hidden, came, dec_gain, n_seq)
        else:
            wide = came.astype(jnp.float32)
            norm = wide * lax.rsqrt(jnp.mean(wide * wide, axis=-1, keepdims=True) + 1e-06) * dec_gain
            norm = norm.astype(jnp.bfloat16).reshape(tok_rows, n_seq, q_rows)
            norm = jnp.moveaxis(norm, 1, 0)
        v["norm"] = (norm, swap(norm, "seq", 1)) if n_core == 2 else (norm,)
        return (norm,)

    @named("keys_values")
    def keys_values(i, mark):
        terms = tuple(after(t, *mark) for t in v["sum", i])
        encoded, *v["kv", i] = project((parts[i],) + terms, key_weight, value_weight)
        if i == 1:
            v["earlier"] = lax.ppermute(
                encoded[piece_rows - key_rows :], "seq", [(i, i + 1) for i in range(n_seq - 1)]
            )
        return tuple(v["kv", i])

    @named("keys_values_earlier")
    def keys_values_earlier(mark):
        v["kv", 2] = project((after(v["earlier"], *mark),), key_weight, value_weight)[1:]
        return tuple(v["kv", 2])

    @named("query_part")
    def query_part(keys, last, mark):
        at = [
            (((z_at - k) % depth) * n_y + (y_at + j) % n_y) * n_core + (core_at + c) % n_core
            for k, j in keys
            for c in range(n_core)
        ]
        norms = tuple(after(n, *mark) for n in v["norm"])
        v["q"] = add_query(
            jnp.stack(at).astype(jnp.int32),
            norms,
            [q_stream.blocks[key] for key in keys],
            v.get("q"),
            jnp.bfloat16 if last else jnp.float32,
        )
        return (v["q"],)

    @named("attention")
    def attention(mark):
        query = v["q"]
        if n_core == 2:
            query = ordered(core_first, query[:tok_rows], swap(query[tok_rows:], "seq", 1), 1)
        grouped = jnp.pad(query, ((1, M - 1), (0, 0)))
        keys, values = zip(v["kv", 2], v["kv", 0], v["kv", 1])
        attn = attend(grouped, keys, values)[1 : tok_rows + 1]
        position = me * tok_rows + jnp.arange(tok_rows, dtype=jnp.int32)[:, None]
        attn = jnp.where(position >= M - 1, attn, jnp.zeros_like(attn))
        v["attn"] = (attn, swap(attn, "seq", 1)) if n_core == 2 else (attn,)
        return (attn,)

    pairs = depth // 2

    @named("scatter")
    def scatter(keys, mark):
        stay = jnp.stack(
            [(((z_at - p) % depth) // pairs == tp_at).astype(jnp.int32) for p, j in keys]
        )
        attns = tuple(after(a, *mark) for a in v["attn"])
        blocks = [((o_stream.blocks[p, j],), (o_stream.blocks[p + pairs, j],)) for p, j in keys]
        sent = out_products(1 - stay, attns, blocks)
        if n_core == 2:
            sent = (sent[0], swap(sent[1], "seq", 1))
        kept = out_products(stay, tuple(after(a, *sent) for a in attns), blocks)
        if n_core == 2:
            kept = (kept[0], swap(kept[1], "seq", 1))
        came = swap(jnp.concatenate(sent, axis=0), "tp", 1)
        for i, key in enumerate(keys):
            v[("piece",) + key] = [
                (kept[c][i], came[c * len(keys) + i]) for c in range(n_core)
            ]
        return (came,) + tuple(kept)

    scatters = n_tp == 2 and depth % 4 == 0
    q, o = q_stream, o_stream
    if depth == 4 and n_y == 2:
        plan = [
            [(q, 1, 0, "on"), (q, 0, 1, "y"), (q, 3, 0, "back"), (o, 0, 1, "y")],
            [(q, 2, 0, "on"), (q, 1, 1, "y"), (o, 1, 0, "on"), (q, 3, 1, "y")],
            [(o, 2, 0, "on"), (q, 2, 1, "y")],
            [(o, 3, 0, "back"), (o, 1, 1, "y")],
            [(o, 3, 1, "back"), (o, 2, 1, "y")],
        ]
    else:
        plan = []
        for k in range(1, depth + 1):
            plan.append([(s, k, 0, "on") for s in (q, o) if k < depth])
            plan[-1] += [(s, k - 1, 1, "y") for s in (q, o) if n_y == 2]
        plan.append([])
    last_query = 1 + max(i for i, moves in enumerate(plan) if any(m[0] is q for m in moves))
    arrived = [(q, 0, 0), (o, 0, 0)]
    asked, made = set(), set()
    token = after(jnp.float32(0), q.blocks[0, 0])
    for phase, moves in enumerate(plan):
        mark = (token,) if phase else ()
        for s, k, j, way in moves:
            s.fetch(k, j, way, mark)
        mark = (token,)
        values = ()
        if phase == 0:
            values += encode(0, mark) + encode_sum(0, mark) + encode(1, mark) + (hidden_came,)
        elif phase == 1:
            values += decode(mark) + keys_values(0, mark) + encode_sum(1, v["norm"])
        elif phase == 2:
            values += keys_values(1, mark)
        elif phase == 3:
            values += keys_values_earlier(mark)
        if 1 <= phase <= last_query:
            keys = [(k, j) for s, k, j in arrived if s is q and (k, j) not in asked]
            asked.update(keys)
            values += query_part(keys, phase == last_query, mark)
        if phase == last_query:
            values += attention(mark)
        if phase > last_query and scatters:
            keys = [(p, j) for p in range(pairs) for j in range(n_y)]
            keys = [
                key
                for key in keys
                if key not in made and {(o,) + key, (o, key[0] + pairs, key[1])} <= set(arrived)
            ]
            if keys:
                made.update(keys)
                values += scatter(keys, mark)
        arrived += [m[:3] for m in moves]
        token = after(token, *(s.blocks[k, j] for s, k, j, _ in moves), *values)

    if scatters:
        order = [(p, j) for p in range(pairs) for j in range(n_y)]
        rest = [key for key in order if key not in made]
        if rest:
            scatter(rest, (token,))
        out = hidden
        for p, j in sorted(order, key=lambda key: key in rest):
            for c, (kept, came) in enumerate(v["piece", p, j]):
                first = (((z_at - p) % pairs) * n_y + (y_at + j) % n_y) * n_core
                first = (first + (core_at + c) % n_core) * o_cols
                branch = kept.astype(jnp.float32) + came.astype(jnp.float32)
                here = lax.dynamic_slice(hidden, (0, first), (tok_rows, o_cols)).astype(jnp.float32)
                out = lax.dynamic_update_slice(out, (here + branch).astype(jnp.bfloat16), (0, first))
        return out

    made = []
    attn = jnp.concatenate(v["attn"], axis=0)
    for k in range(depth):
        for j in range(n_y):
            total = jnp.dot(attn, o_stream.blocks[k, j], preferred_element_type=jnp.float32)
            made.append(total.astype(jnp.bfloat16))
    made = jnp.stack(made, axis=0)[:, None]
    if n_core == 2:
        theirs = swap(made[:, :, tok_rows:], "seq", 1)
        made = jnp.concatenate([made[:, :, :tok_rows], theirs], axis=1)
    made = made.reshape(n_seq, tok_rows, o_cols)
    block = jnp.arange(n_seq, dtype=jnp.int32)
    b_z, b_y, b_c = block // (n_y * n_core), (block // n_core) % n_y, block % n_core
    at = (((z_at - b_z) % depth) * n_y + (b_y - y_at) % n_y) * n_core + (b_c - core_at) % n_core
    whole = jnp.moveaxis(jnp.take(made, at, axis=0), 0, 1).reshape(tok_rows, feat * n_tp)
    branch = lax.psum_scatter(whole, "tp", scatter_dimension=1, tiled=True).astype(jnp.float32)
    return (hidden.astype(jnp.float32) + branch).astype(jnp.bfloat16)


def solution(mesh):
    placed = (
        P("seq", "tp"),
        P("seq", None, None),
        P(),
        P(None, "tp"),
        P("tp", None),
        P(None, "tp"),
        P(None, "tp"),
        P(),
        P("seq", "tp"),
        P("tp", "seq"),
    )
    return jax.shard_map(
        per_device, mesh=mesh, in_specs=placed, out_specs=P("seq", "tp"), check_vma=False
    )
```

```python
import functools

import jax
import jax.numpy as jnp
from jax import lax
from jax.experimental import pallas as pl
from jax.experimental.pallas import tpu as pltpu
from jax.sharding import PartitionSpec as P

HD = 128
M = 64
KEYS = 256


def factors(count):
    core = 2 if count % 2 == 0 else 1
    y = 2 if (count // core) % 2 == 0 else 1
    return count // (core * y), y, core


def swap(value, axis, stride):
    count = lax.axis_size(axis)
    pairs = [(i, i + stride if (i // stride) % 2 == 0 else i - stride) for i in range(count)]
    return lax.ppermute(value, axis, pairs)


def ring(value, axis, stride):
    count = lax.axis_size(axis)
    return lax.ppermute(value, axis, [(i, (i + stride) % count) for i in range(count)])


def named(name):
    def wrap(function):
        def inner(*args):
            with jax.named_scope(name):
                return function(*args)

        return inner

    return wrap


def after(value, *done):
    return lax.optimization_barrier((value,) + done)[0]


class Stream:
    def __init__(self, name, block):
        self.depth, self.n_y, self.n_core = factors(lax.axis_size("seq"))
        self.name, self.blocks = name, {(0, 0): block}

    def fetch(self, k, j, way, mark):
        step = self.n_core * self.n_y
        with jax.named_scope(f"{self.name}_{k}_{j}"):
            if way == "y":
                made = swap(after(self.blocks[k, 0], *mark), "seq", self.n_core)
            elif way == "on":
                made = ring(after(self.blocks[k - 1, j], *mark), "seq", step)
            else:
                made = ring(after(self.blocks[(k + 1) % self.depth, j], *mark), "seq", -step)
        self.blocks[k, j] = made


def ordered(flag, first, second, axis):
    return jnp.concatenate(
        [jnp.where(flag, first, second), jnp.where(flag, second, first)], axis=axis
    )


WHOLE = pl.BlockSpec(memory_space=pltpu.VMEM)
SCALARS = pl.BlockSpec(memory_space=pltpu.SMEM)


def cost(flops, moved):
    return pl.CostEstimate(flops=int(flops), bytes_accessed=int(moved), transcendentals=0)


def params(mib):
    return pltpu.CompilerParams(vmem_limit_bytes=mib * 1024 * 1024)


def tiles(size, tile=256):
    return tile if size % tile == 0 else size


def encode_kernel(x_ref, gain_ref, first_ref, second_ref, out_ref, norm_ref, inner_ref):
    x = x_ref[...].astype(jnp.float32)
    scale = lax.rsqrt(jnp.mean(x * x, axis=-1, keepdims=True) + 1e-06)
    norm_ref[...] = (x * scale * gain_ref[...]).astype(jnp.bfloat16)
    units = first_ref.shape[1]
    tile = tiles(units)
    for n in range(0, units, tile):
        made = jnp.dot(norm_ref[...], first_ref[:, n : n + tile], preferred_element_type=jnp.float32)
        inner_ref[:, n : n + tile] = jnp.maximum(made, 0.0).astype(jnp.bfloat16)
    rows = tiles(x_ref.shape[0])
    for m in range(0, x_ref.shape[0], rows):
        out_ref[m : m + rows, :] = jnp.dot(
            inner_ref[m : m + rows, :], second_ref[...], preferred_element_type=jnp.float32
        ).astype(jnp.bfloat16)


def encode_partial(tokens, gain, first_weight, second_weight):
    rows = tokens.shape[0]
    return pl.pallas_call(
        encode_kernel,
        in_specs=[WHOLE] * 4,
        out_specs=WHOLE,
        out_shape=jax.ShapeDtypeStruct((rows, second_weight.shape[1]), jnp.bfloat16),
        scratch_shapes=[
            pltpu.VMEM(tokens.shape, jnp.bfloat16),
            pltpu.VMEM((rows, first_weight.shape[1]), jnp.bfloat16),
        ],
        compiler_params=params(14),
        cost_estimate=cost(4 * rows * tokens.shape[1] * first_weight.shape[1], 4 * first_weight.size),
        name="encode",
    )(tokens, gain, first_weight, second_weight)


def project_kernel(terms, *refs):
    part_refs, (k_in, v_in, enc_ref, k_ref, v_ref) = refs[:terms], refs[terms:]
    total = part_refs[0][...].astype(jnp.float32)
    if terms > 1:
        summed = part_refs[1][...].astype(jnp.float32)
        for ref in part_refs[2:]:
            summed = summed + ref[...].astype(jnp.float32)
        total = total + summed
    enc_ref[...] = total.astype(jnp.bfloat16)
    cols = k_in.shape[1]
    tile = tiles(cols)
    for w_ref, o_ref in ((k_in, k_ref), (v_in, v_ref)):
        for n in range(0, cols, tile):
            o_ref[:, n : n + tile] = jnp.dot(
                enc_ref[...], w_ref[:, n : n + tile], preferred_element_type=jnp.float32
            ).astype(jnp.bfloat16)


def project(parts, key_weight, value_weight):
    rows, width = parts[0].shape
    cols = key_weight.shape[1]
    return pl.pallas_call(
        functools.partial(project_kernel, len(parts)),
        in_specs=[WHOLE] * (len(parts) + 2),
        out_specs=[WHOLE] * 3,
        out_shape=[
            jax.ShapeDtypeStruct((rows, width), jnp.bfloat16),
            jax.ShapeDtypeStruct((rows, cols), jnp.bfloat16),
            jax.ShapeDtypeStruct((rows, cols), jnp.bfloat16),
        ],
        compiler_params=params(18),
        cost_estimate=cost(4 * rows * width * cols, 4 * key_weight.size),
        name="project",
    )(*parts, key_weight, value_weight)


def decode_kernel(at_ref, own_ref, came_ref, gain_ref, out_ref):
    own, came = own_ref[...].astype(jnp.float32), came_ref[...].astype(jnp.float32)
    shards, _, width = out_ref.shape
    half = shards // 2
    total = jnp.sum(own * own, axis=-1, keepdims=True) + jnp.sum(came * came, axis=-1, keepdims=True)
    scale = lax.rsqrt(total / (shards * width) + 1e-06)
    for i, ref in enumerate((own_ref, came_ref)):
        for g in range(half):
            to = at_ref[i] + g
            value = ref[:, g * width : (g + 1) * width].astype(jnp.float32)
            out_ref[to] = (value * scale * gain_ref[to]).astype(jnp.bfloat16)


def decode_norm(own_first, own, came, gain, shards):
    rows, half = own.shape
    width = 2 * half // shards
    at = jnp.where(own_first, jnp.array([0, shards // 2]), jnp.array([shards // 2, 0]))
    return pl.pallas_call(
        decode_kernel,
        in_specs=[SCALARS] + [WHOLE] * 3,
        out_specs=WHOLE,
        out_shape=jax.ShapeDtypeStruct((shards, rows, width), jnp.bfloat16),
        compiler_params=params(8),
        cost_estimate=cost(0, 10 * own.size),
        name="decode",
    )(at.astype(jnp.int32), own, came, gain.reshape(shards, 1, width))


def query_kernel(norms, blocks, more, at_ref, *refs):
    norm_refs, block_refs = refs[:norms], refs[norms : norms + blocks]
    out_ref = refs[-1]
    rows, depth = norm_refs[0].shape[1:]
    tile = tiles(out_ref.shape[1])
    for i, norm_ref in enumerate(norm_refs):
        own = slice(i * rows, (i + 1) * rows)
        for n in range(0, out_ref.shape[1], tile):
            cols = slice(n, n + tile)
            total, at = None, 0
            for block_ref in block_refs:
                for first in range(0, block_ref.shape[0], depth):
                    term = jnp.dot(
                        norm_ref[at_ref[at]],
                        block_ref[first : first + depth, cols],
                        preferred_element_type=jnp.float32,
                    )
                    total, at = term if total is None else total + term, at + 1
            if more:
                total = total + refs[-2][own, cols]
            out_ref[own, cols] = total.astype(out_ref.dtype)


def add_query(at, norms, blocks, total, dtype):
    more = () if total is None else (total,)
    shape = (len(norms) * norms[0].shape[1], blocks[0].shape[1])
    moved = sum(b.size for b in blocks)
    return pl.pallas_call(
        functools.partial(query_kernel, len(norms), len(blocks), len(more)),
        in_specs=[SCALARS] + [WHOLE] * (len(norms) + len(blocks) + len(more)),
        out_specs=WHOLE,
        out_shape=jax.ShapeDtypeStruct(shape, dtype),
        compiler_params=params(18),
        cost_estimate=cost(2 * shape[0] * moved, 2 * moved),
        name="query",
    )(at, *norms, *blocks, *more)


def out_kernel(attns, sizes, near_ref, *refs):
    attn_refs, block_refs, out_refs = refs[:attns], refs[attns:-attns], refs[-attns:]
    first = 0
    for i, counts in enumerate(sizes):
        for branch, count in enumerate(counts):
            parts = block_refs[first : first + count]
            first += count

            @pl.when(near_ref[i] == 1 - branch)
            def _(i=i, parts=parts):
                for attn_ref, out_ref in zip(attn_refs, out_refs):
                    total, row = None, 0
                    for ref in parts:
                        size = ref.shape[0]
                        term = jnp.dot(
                            attn_ref[:, row : row + size],
                            ref[...],
                            preferred_element_type=jnp.float32,
                        )
                        total, row = term if total is None else total + term, row + size
                    out_ref[i] = total.astype(jnp.bfloat16)


def out_products(near, attns, pairs):
    shape = jax.ShapeDtypeStruct(
        (len(pairs), attns[0].shape[0], pairs[0][0][0].shape[1]), jnp.bfloat16
    )
    flat = [part for pair in pairs for block in pair for part in block]
    return pl.pallas_call(
        functools.partial(out_kernel, len(attns), [[len(b) for b in pair] for pair in pairs]),
        in_specs=[SCALARS] + [WHOLE] * (len(attns) + len(flat)),
        out_specs=[WHOLE] * len(attns),
        out_shape=[shape] * len(attns),
        compiler_params=params(14),
        cost_estimate=cost(0, 1024),
        name="out",
    )(near, *attns, *flat)


def attend_kernel(heads, pieces, q_ref, *refs):
    k_refs, v_refs, o_ref = refs[: len(pieces)], refs[len(pieces) : -1], refs[-1]
    scale = HD ** (-0.5)
    units = [(p, s) for p, count in enumerate(pieces) for s in range(count)]
    for h in range(heads):
        cols = slice(h * HD, (h + 1) * HD)
        scores = []
        for u, (p, s) in enumerate(units):
            scores.append(
                lax.dot_general(
                    q_ref[u * M : (u + 1) * M, cols],
                    k_refs[p][s * KEYS : (s + 1) * KEYS, cols],
                    (((1,), (1,)), ((), ())),
                    preferred_element_type=jnp.float32,
                )
            )
        tops = [jnp.max(s, axis=-1, keepdims=True) for s in scores]
        exps = [jnp.exp((s - t) * scale) for s, t in zip(scores, tops)]
        scales = [1.0 / jnp.sum(e, axis=-1, keepdims=True) for e in exps]
        probs = [(e * r).astype(jnp.bfloat16) for e, r in zip(exps, scales)]
        for u, (p, s) in enumerate(units):
            o_ref[u * M : (u + 1) * M, cols] = jnp.dot(
                probs[u],
                v_refs[p][s * KEYS : (s + 1) * KEYS, cols],
                preferred_element_type=jnp.float32,
            ).astype(jnp.bfloat16)


def attend(query, keys, values):
    rows, width = query.shape
    heads = 2 if (width // HD) % 2 == 0 else 1
    block = heads * HD
    pieces = tuple(k.shape[0] // KEYS for k in keys)
    held = [pl.BlockSpec((k.shape[0], block), lambda i: (0, i)) for k in keys]
    return pl.pallas_call(
        functools.partial(attend_kernel, heads, pieces),
        grid=(width // block,),
        in_specs=[pl.BlockSpec((rows, block), lambda i: (0, i))] + held + held,
        out_specs=pl.BlockSpec((rows, block), lambda i: (0, i)),
        out_shape=jax.ShapeDtypeStruct((rows, width), jnp.bfloat16),
        compiler_params=params(10),
        cost_estimate=cost(0, 1024),
        name="attend",
    )(query, *keys, *values)


def per_device(
    hidden,
    neighbours,
    enc_gain,
    enc_w1,
    enc_w2,
    key_weight,
    value_weight,
    dec_gain,
    query_weight,
    out_weight,
):
    tok_rows, feat = hidden.shape
    span_count, key_rows, width = neighbours.shape
    n_seq, n_tp = lax.axis_size("seq"), lax.axis_size("tp")
    depth, n_y, n_core = factors(n_seq)
    me = lax.axis_index("seq")
    tp_at = lax.axis_index("tp")
    core_at, y_at, z_at = me % n_core, (me // n_core) % n_y, me // (n_core * n_y)
    core_first = core_at == 0

    q_rows, q_cols = query_weight.shape
    per_core = q_cols // n_core
    block = lax.dynamic_slice(query_weight, (0, core_at * per_core), (q_rows, per_core))
    if n_core == 2:
        theirs = lax.dynamic_slice(query_weight, (0, (1 - core_at) * per_core), (q_rows, per_core))
        block = jnp.concatenate([block, swap(theirs, "seq", 1)], axis=0)
    q_stream = Stream("query", block)

    o_rows, o_cols = out_weight.shape
    o_stream = Stream("out", out_weight)

    if n_tp == 2:
        hidden_came = swap(hidden, "tp", 1)
    else:
        hidden_came = lax.all_gather(hidden, "tp", axis=1, tiled=True)

    flat = neighbours.reshape(span_count * key_rows, width)
    piece_rows = flat.shape[0] // 2
    parts = [flat[i * piece_rows : (i + 1) * piece_rows] for i in range(2)]
    gain = enc_gain.reshape(1, width)
    v = {}

    @named("encode")
    def encode(i, mark):
        v["part", i] = encode_partial(after(parts[i], *mark), gain, enc_w1, enc_w2)
        return (v["part", i],)

    @named("encode_sum")
    def encode_sum(i, mark):
        own = after(v["part", i], *mark)
        if n_tp == 2:
            v["sum", i] = (own, swap(own, "tp", 1))
        else:
            v["sum", i] = (lax.psum(own, "tp"),)
        return v["sum", i]

    @named("decode")
    def decode(mark):
        came = after(hidden_came, *mark)
        if n_tp == 2:
            norm = decode_norm(tp_at == 0, hidden, came, dec_gain, n_seq)
        else:
            wide = came.astype(jnp.float32)
            norm = wide * lax.rsqrt(jnp.mean(wide * wide, axis=-1, keepdims=True) + 1e-06) * dec_gain
            norm = norm.astype(jnp.bfloat16).reshape(tok_rows, n_seq, q_rows)
            norm = jnp.moveaxis(norm, 1, 0)
        v["norm"] = (norm, swap(norm, "seq", 1)) if n_core == 2 else (norm,)
        return (norm,)

    @named("keys_values")
    def keys_values(i, mark):
        terms = tuple(after(t, *mark) for t in v["sum", i])
        encoded, *v["kv", i] = project((parts[i],) + terms, key_weight, value_weight)
        if i == 1:
            v["earlier"] = lax.ppermute(
                encoded[piece_rows - key_rows :], "seq", [(i, i + 1) for i in range(n_seq - 1)]
            )
        return tuple(v["kv", i])

    @named("keys_values_earlier")
    def keys_values_earlier(mark):
        v["kv", 2] = project((after(v["earlier"], *mark),), key_weight, value_weight)[1:]
        return tuple(v["kv", 2])

    @named("query_part")
    def query_part(keys, last, mark):
        at = [
            (((z_at - k) % depth) * n_y + (y_at + j) % n_y) * n_core + (core_at + c) % n_core
            for k, j in keys
            for c in range(n_core)
        ]
        norms = tuple(after(n, *mark) for n in v["norm"])
        v["q"] = add_query(
            jnp.stack(at).astype(jnp.int32),
            norms,
            [q_stream.blocks[key] for key in keys],
            v.get("q"),
            jnp.bfloat16 if last else jnp.float32,
        )
        return (v["q"],)

    @named("attention")
    def attention(mark):
        query = v["q"]
        if n_core == 2:
            query = ordered(core_first, query[:tok_rows], swap(query[tok_rows:], "seq", 1), 1)
        grouped = jnp.pad(query, ((1, M - 1), (0, 0)))
        keys, values = zip(v["kv", 2], v["kv", 0], v["kv", 1])
        attn = attend(grouped, keys, values)[1 : tok_rows + 1]
        position = me * tok_rows + jnp.arange(tok_rows, dtype=jnp.int32)[:, None]
        attn = jnp.where(position >= M - 1, attn, jnp.zeros_like(attn))
        v["attn"] = (attn, swap(attn, "seq", 1)) if n_core == 2 else (attn,)
        return (attn,)

    pairs = depth // 2

    def out_part(keys, away, mark):
        stay = jnp.stack(
            [(((z_at - p) % depth) // pairs == tp_at).astype(jnp.int32) for p, j in keys]
        )
        attns = tuple(after(a, *mark) for a in v["attn"])
        blocks = [((o_stream.blocks[p, j],), (o_stream.blocks[p + pairs, j],)) for p, j in keys]
        made = out_products(1 - stay if away else stay, attns, blocks)
        return (made[0], swap(made[1], "seq", 1)) if n_core == 2 else made

    @named("send")
    def send(keys, mark):
        sent = out_part(keys, True, mark)
        came = swap(jnp.concatenate(sent, axis=0), "tp", 1)
        for i, key in enumerate(keys):
            v[("came",) + key] = [came[c * len(keys) + i] for c in range(n_core)]
        return (came,), tuple(sent)

    @named("keep")
    def keep(keys, mark):
        kept = out_part(keys, False, mark)
        for i, key in enumerate(keys):
            v[("piece",) + key] = [(kept[c][i], v[("came",) + key][c]) for c in range(n_core)]
        return tuple(kept)

    v["mixed"] = hidden

    def place(keys):
        for p, j in keys:
            first = (((z_at - p) % pairs) * n_y + (y_at + j) % n_y) * n_core * o_cols
            sums = [
                kept.astype(jnp.float32) + came.astype(jnp.float32) for kept, came in v["piece", p, j]
            ]
            branch = ordered(core_first, *sums, 1) if n_core == 2 else sums[0]
            here = lax.dynamic_slice(hidden, (0, first), branch.shape).astype(jnp.float32)
            v["mixed"] = lax.dynamic_update_slice(
                v["mixed"], (here + branch).astype(jnp.bfloat16), (0, first)
            )

    scatters = n_tp == 2 and depth % 4 == 0
    q, o = q_stream, o_stream
    if depth == 4 and n_y == 2:
        plan = [
            [(q, 1, 0, "on"), (q, 0, 1, "y"), (q, 3, 0, "back"), (o, 0, 1, "y")],
            [(q, 2, 0, "on"), (q, 1, 1, "y"), (o, 1, 0, "on"), (q, 3, 1, "y")],
            [(o, 2, 0, "on"), (q, 2, 1, "y")],
            [(o, 3, 0, "back"), (o, 2, 1, "y")],
            [(o, 3, 1, "back"), (o, 1, 1, "y")],
        ]
    else:
        plan = []
        for k in range(1, depth + 1):
            plan.append([(s, k, 0, "on") for s in (q, o) if k < depth])
            plan[-1] += [(s, k - 1, 1, "y") for s in (q, o) if n_y == 2]
        plan.append([])
    last_query = 1 + max(i for i, moves in enumerate(plan) if any(m[0] is q for m in moves))
    arrived = [(q, 0, 0), (o, 0, 0)]
    asked, made = set(), set()
    token = after(jnp.float32(0), q.blocks[0, 0])
    for phase, moves in enumerate(plan):
        mark = (token,) if phase else ()
        for s, k, j, way in moves:
            s.fetch(k, j, way, mark)
        mark = (token,)
        values = ()
        if phase == 0:
            values += encode(0, mark) + encode_sum(0, mark) + encode(1, mark) + (hidden_came,)
        elif phase == 1:
            values += decode(mark) + keys_values(0, mark) + encode_sum(1, v["norm"])
        elif phase == 2:
            values += keys_values(1, mark)
        elif phase == 3:
            values += keys_values_earlier(mark)
        if 1 <= phase <= last_query:
            keys = [(k, j) for s, k, j in arrived if s is q and (k, j) not in asked]
            asked.update(keys)
            values += query_part(keys, phase == last_query, mark)
        if phase == last_query:
            values += attention(mark)
        if phase > last_query and scatters:
            keys = [(p, j) for p in range(pairs) for j in range(n_y)]
            keys = [
                key
                for key in keys
                if key not in made and {(o,) + key, (o, key[0] + pairs, key[1])} <= set(arrived)
            ]
            first = ()
            for j in range(n_y):
                here = [key for key in keys if key[1] == j]
                if here:
                    made.update(here)
                    came, _ = send(here, mark)
                    values += came
                    first = first or came
            if keys:
                keep(keys, first)
        arrived += [m[:3] for m in moves]
        token = after(token, *(s.blocks[k, j] for s, k, j, _ in moves), *values)

    if scatters:
        order = [(p, j) for p in range(pairs) for j in range(n_y)]
        rest = [key for key in order if key not in made]
        sent = send(rest, (token,))[1] if rest else ()
        waiting = [key for key in order if key not in rest and ("piece",) + key not in v]
        if waiting:
            keep(waiting, (token,) + sent)
        place([key for key in order if key not in rest])
        if rest:
            keep(rest, sent)
            place(rest)
        return v["mixed"]

    made = []
    attn = jnp.concatenate(v["attn"], axis=0)
    for k in range(depth):
        for j in range(n_y):
            total = jnp.dot(attn, o_stream.blocks[k, j], preferred_element_type=jnp.float32)
            made.append(total.astype(jnp.bfloat16))
    made = jnp.stack(made, axis=0)[:, None]
    if n_core == 2:
        theirs = swap(made[:, :, tok_rows:], "seq", 1)
        made = jnp.concatenate([made[:, :, :tok_rows], theirs], axis=1)
    made = made.reshape(n_seq, tok_rows, o_cols)
    block = jnp.arange(n_seq, dtype=jnp.int32)
    b_z, b_y, b_c = block // (n_y * n_core), (block // n_core) % n_y, block % n_core
    at = (((z_at - b_z) % depth) * n_y + (b_y - y_at) % n_y) * n_core + (b_c - core_at) % n_core
    whole = jnp.moveaxis(jnp.take(made, at, axis=0), 0, 1).reshape(tok_rows, feat * n_tp)
    branch = lax.psum_scatter(whole, "tp", scatter_dimension=1, tiled=True).astype(jnp.float32)
    return (hidden.astype(jnp.float32) + branch).astype(jnp.bfloat16)


def solution(mesh):
    placed = (
        P("seq", "tp"),
        P("seq", None, None),
        P(),
        P(None, "tp"),
        P("tp", None),
        P(None, "tp"),
        P(None, "tp"),
        P(),
        P("seq", "tp"),
        P("tp", "seq"),
    )
    return jax.shard_map(
        per_device, mesh=mesh, in_specs=placed, out_specs=P("seq", "tp"), check_vma=False
    )
```

```python
import functools

import jax
import jax.numpy as jnp
from jax import lax
from jax.experimental import pallas as pl
from jax.experimental.pallas import tpu as pltpu
from jax.sharding import PartitionSpec as P

HD = 128
M = 64
KEYS = 256


def factors(count):
    core = 2 if count % 2 == 0 else 1
    y = 2 if (count // core) % 2 == 0 else 1
    return count // (core * y), y, core


def swap(value, axis, stride):
    count = lax.axis_size(axis)
    pairs = [(i, i + stride if (i // stride) % 2 == 0 else i - stride) for i in range(count)]
    return lax.ppermute(value, axis, pairs)


def ring(value, axis, stride):
    count = lax.axis_size(axis)
    return lax.ppermute(value, axis, [(i, (i + stride) % count) for i in range(count)])


def named(name):
    def wrap(function):
        def inner(*args):
            with jax.named_scope(name):
                return function(*args)

        return inner

    return wrap


def after(value, *done):
    return lax.optimization_barrier((value,) + done)[0]


class Stream:
    def __init__(self, name, block):
        self.depth, self.n_y, self.n_core = factors(lax.axis_size("seq"))
        self.name, self.blocks = name, {(0, 0): block}

    def fetch(self, k, j, way, mark):
        step = self.n_core * self.n_y
        with jax.named_scope(f"{self.name}_{k}_{j}"):
            if way == "y":
                made = swap(after(self.blocks[k, 0], *mark), "seq", self.n_core)
            elif way == "on":
                made = ring(after(self.blocks[k - 1, j], *mark), "seq", step)
            else:
                made = ring(after(self.blocks[(k + 1) % self.depth, j], *mark), "seq", -step)
        self.blocks[k, j] = made


def ordered(flag, first, second, axis):
    return jnp.concatenate(
        [jnp.where(flag, first, second), jnp.where(flag, second, first)], axis=axis
    )


WHOLE = pl.BlockSpec(memory_space=pltpu.VMEM)
SCALARS = pl.BlockSpec(memory_space=pltpu.SMEM)


def cost(flops, moved):
    return pl.CostEstimate(flops=int(flops), bytes_accessed=int(moved), transcendentals=0)


def params(mib):
    return pltpu.CompilerParams(vmem_limit_bytes=mib * 1024 * 1024)


def tiles(size, tile=256):
    return tile if size % tile == 0 else size


def encode_kernel(x_ref, gain_ref, first_ref, second_ref, out_ref, norm_ref, inner_ref):
    x = x_ref[...].astype(jnp.float32)
    scale = lax.rsqrt(jnp.mean(x * x, axis=-1, keepdims=True) + 1e-06)
    norm_ref[...] = (x * scale * gain_ref[...]).astype(jnp.bfloat16)
    units = first_ref.shape[1]
    tile = tiles(units)
    for n in range(0, units, tile):
        made = jnp.dot(norm_ref[...], first_ref[:, n : n + tile], preferred_element_type=jnp.float32)
        inner_ref[:, n : n + tile] = jnp.maximum(made, 0.0).astype(jnp.bfloat16)
    rows = tiles(x_ref.shape[0])
    for m in range(0, x_ref.shape[0], rows):
        out_ref[m : m + rows, :] = jnp.dot(
            inner_ref[m : m + rows, :], second_ref[...], preferred_element_type=jnp.float32
        ).astype(jnp.bfloat16)


def encode_partial(tokens, gain, first_weight, second_weight):
    rows = tokens.shape[0]
    return pl.pallas_call(
        encode_kernel,
        in_specs=[WHOLE] * 4,
        out_specs=WHOLE,
        out_shape=jax.ShapeDtypeStruct((rows, second_weight.shape[1]), jnp.bfloat16),
        scratch_shapes=[
            pltpu.VMEM(tokens.shape, jnp.bfloat16),
            pltpu.VMEM((rows, first_weight.shape[1]), jnp.bfloat16),
        ],
        compiler_params=params(14),
        cost_estimate=cost(4 * rows * tokens.shape[1] * first_weight.shape[1], 4 * first_weight.size),
        name="encode",
    )(tokens, gain, first_weight, second_weight)


def project_kernel(terms, *refs):
    part_refs, (k_in, v_in, enc_ref, k_ref, v_ref) = refs[:terms], refs[terms:]
    total = part_refs[0][...].astype(jnp.float32)
    if terms > 1:
        summed = part_refs[1][...].astype(jnp.float32)
        for ref in part_refs[2:]:
            summed = summed + ref[...].astype(jnp.float32)
        total = total + summed
    enc_ref[...] = total.astype(jnp.bfloat16)
    cols = k_in.shape[1]
    tile = tiles(cols)
    for w_ref, o_ref in ((k_in, k_ref), (v_in, v_ref)):
        for n in range(0, cols, tile):
            o_ref[:, n : n + tile] = jnp.dot(
                enc_ref[...], w_ref[:, n : n + tile], preferred_element_type=jnp.float32
            ).astype(jnp.bfloat16)


def project(parts, key_weight, value_weight):
    rows, width = parts[0].shape
    cols = key_weight.shape[1]
    return pl.pallas_call(
        functools.partial(project_kernel, len(parts)),
        in_specs=[WHOLE] * (len(parts) + 2),
        out_specs=[WHOLE] * 3,
        out_shape=[
            jax.ShapeDtypeStruct((rows, width), jnp.bfloat16),
            jax.ShapeDtypeStruct((rows, cols), jnp.bfloat16),
            jax.ShapeDtypeStruct((rows, cols), jnp.bfloat16),
        ],
        compiler_params=params(18),
        cost_estimate=cost(4 * rows * width * cols, 4 * key_weight.size),
        name="project",
    )(*parts, key_weight, value_weight)


def decode_kernel(at_ref, own_ref, came_ref, gain_ref, out_ref):
    own, came = own_ref[...].astype(jnp.float32), came_ref[...].astype(jnp.float32)
    shards, _, width = out_ref.shape
    half = shards // 2
    total = jnp.sum(own * own, axis=-1, keepdims=True) + jnp.sum(came * came, axis=-1, keepdims=True)
    scale = lax.rsqrt(total / (shards * width) + 1e-06)
    for i, ref in enumerate((own_ref, came_ref)):
        for g in range(half):
            to = at_ref[i] + g
            value = ref[:, g * width : (g + 1) * width].astype(jnp.float32)
            out_ref[to] = (value * scale * gain_ref[to]).astype(jnp.bfloat16)


def decode_norm(own_first, own, came, gain, shards):
    rows, half = own.shape
    width = 2 * half // shards
    at = jnp.where(own_first, jnp.array([0, shards // 2]), jnp.array([shards // 2, 0]))
    return pl.pallas_call(
        decode_kernel,
        in_specs=[SCALARS] + [WHOLE] * 3,
        out_specs=WHOLE,
        out_shape=jax.ShapeDtypeStruct((shards, rows, width), jnp.bfloat16),
        compiler_params=params(8),
        cost_estimate=cost(0, 10 * own.size),
        name="decode",
    )(at.astype(jnp.int32), own, came, gain.reshape(shards, 1, width))


def query_kernel(norms, blocks, more, at_ref, *refs):
    norm_refs, block_refs = refs[:norms], refs[norms : norms + blocks]
    out_ref = refs[-1]
    rows, depth = norm_refs[0].shape[1:]
    tile = tiles(out_ref.shape[1])
    for i, norm_ref in enumerate(norm_refs):
        own = slice(i * rows, (i + 1) * rows)
        for n in range(0, out_ref.shape[1], tile):
            cols = slice(n, n + tile)
            total, at = None, 0
            for block_ref in block_refs:
                for first in range(0, block_ref.shape[0], depth):
                    term = jnp.dot(
                        norm_ref[at_ref[at]],
                        block_ref[first : first + depth, cols],
                        preferred_element_type=jnp.float32,
                    )
                    total, at = term if total is None else total + term, at + 1
            if more:
                total = total + refs[-2][own, cols]
            out_ref[own, cols] = total.astype(out_ref.dtype)


def add_query(at, norms, blocks, total, dtype):
    more = () if total is None else (total,)
    shape = (len(norms) * norms[0].shape[1], blocks[0].shape[1])
    moved = sum(b.size for b in blocks)
    return pl.pallas_call(
        functools.partial(query_kernel, len(norms), len(blocks), len(more)),
        in_specs=[SCALARS] + [WHOLE] * (len(norms) + len(blocks) + len(more)),
        out_specs=WHOLE,
        out_shape=jax.ShapeDtypeStruct(shape, dtype),
        compiler_params=params(18),
        cost_estimate=cost(2 * shape[0] * moved, 2 * moved),
        name="query",
    )(at, *norms, *blocks, *more)


def out_kernel(attns, sizes, near_ref, *refs):
    attn_refs, block_refs, out_refs = refs[:attns], refs[attns:-attns], refs[-attns:]
    first = 0
    for i, counts in enumerate(sizes):
        for branch, count in enumerate(counts):
            parts = block_refs[first : first + count]
            first += count

            @pl.when(near_ref[i] == 1 - branch)
            def _(i=i, parts=parts):
                for attn_ref, out_ref in zip(attn_refs, out_refs):
                    total, row = None, 0
                    for ref in parts:
                        size = ref.shape[0]
                        term = jnp.dot(
                            attn_ref[:, row : row + size],
                            ref[...],
                            preferred_element_type=jnp.float32,
                        )
                        total, row = term if total is None else total + term, row + size
                    out_ref[i] = total.astype(jnp.bfloat16)


def out_products(near, attns, pairs):
    shape = jax.ShapeDtypeStruct(
        (len(pairs), attns[0].shape[0], pairs[0][0][0].shape[1]), jnp.bfloat16
    )
    flat = [part for pair in pairs for block in pair for part in block]
    return pl.pallas_call(
        functools.partial(out_kernel, len(attns), [[len(b) for b in pair] for pair in pairs]),
        in_specs=[SCALARS] + [WHOLE] * (len(attns) + len(flat)),
        out_specs=[WHOLE] * len(attns),
        out_shape=[shape] * len(attns),
        compiler_params=params(14),
        cost_estimate=cost(0, 1024),
        name="out",
    )(near, *attns, *flat)


def attend_kernel(heads, pieces, q_ref, *refs):
    k_refs, v_refs, o_ref = refs[: len(pieces)], refs[len(pieces) : -1], refs[-1]
    scale = HD ** (-0.5)
    units = [(p, s) for p, count in enumerate(pieces) for s in range(count)]
    for h in range(heads):
        cols = slice(h * HD, (h + 1) * HD)
        scores = []
        for u, (p, s) in enumerate(units):
            scores.append(
                lax.dot_general(
                    q_ref[u * M : (u + 1) * M, cols],
                    k_refs[p][s * KEYS : (s + 1) * KEYS, cols],
                    (((1,), (1,)), ((), ())),
                    preferred_element_type=jnp.float32,
                )
            )
        tops = [jnp.max(s, axis=-1, keepdims=True) for s in scores]
        exps = [jnp.exp((s - t) * scale) for s, t in zip(scores, tops)]
        scales = [1.0 / jnp.sum(e, axis=-1, keepdims=True) for e in exps]
        probs = [(e * r).astype(jnp.bfloat16) for e, r in zip(exps, scales)]
        for u, (p, s) in enumerate(units):
            o_ref[u * M : (u + 1) * M, cols] = jnp.dot(
                probs[u],
                v_refs[p][s * KEYS : (s + 1) * KEYS, cols],
                preferred_element_type=jnp.float32,
            ).astype(jnp.bfloat16)


def attend(query, keys, values):
    rows, width = query.shape
    heads = 2 if (width // HD) % 2 == 0 else 1
    block = heads * HD
    pieces = tuple(k.shape[0] // KEYS for k in keys)
    held = [pl.BlockSpec((k.shape[0], block), lambda i: (0, i)) for k in keys]
    return pl.pallas_call(
        functools.partial(attend_kernel, heads, pieces),
        grid=(width // block,),
        in_specs=[pl.BlockSpec((rows, block), lambda i: (0, i))] + held + held,
        out_specs=pl.BlockSpec((rows, block), lambda i: (0, i)),
        out_shape=jax.ShapeDtypeStruct((rows, width), jnp.bfloat16),
        compiler_params=params(10),
        cost_estimate=cost(0, 1024),
        name="attend",
    )(query, *keys, *values)


def per_device(
    hidden,
    neighbours,
    enc_gain,
    enc_w1,
    enc_w2,
    key_weight,
    value_weight,
    dec_gain,
    query_weight,
    out_weight,
):
    tok_rows, feat = hidden.shape
    span_count, key_rows, width = neighbours.shape
    n_seq, n_tp = lax.axis_size("seq"), lax.axis_size("tp")
    depth, n_y, n_core = factors(n_seq)
    me = lax.axis_index("seq")
    tp_at = lax.axis_index("tp")
    core_at, y_at, z_at = me % n_core, (me // n_core) % n_y, me // (n_core * n_y)
    core_first = core_at == 0

    q_rows, q_cols = query_weight.shape
    per_core = q_cols // n_core
    block = lax.dynamic_slice(query_weight, (0, core_at * per_core), (q_rows, per_core))
    if n_core == 2:
        theirs = lax.dynamic_slice(query_weight, (0, (1 - core_at) * per_core), (q_rows, per_core))
        block = jnp.concatenate([block, swap(theirs, "seq", 1)], axis=0)
    q_stream = Stream("query", block)

    o_rows, o_cols = out_weight.shape
    o_stream = Stream("out", out_weight)

    if n_tp == 2:
        hidden_came = swap(hidden, "tp", 1)
    else:
        hidden_came = lax.all_gather(hidden, "tp", axis=1, tiled=True)

    flat = neighbours.reshape(span_count * key_rows, width)
    piece_rows = flat.shape[0] // 2
    parts = [flat[i * piece_rows : (i + 1) * piece_rows] for i in range(2)]
    gain = enc_gain.reshape(1, width)
    v = {}

    @named("encode")
    def encode(i, mark):
        v["part", i] = encode_partial(after(parts[i], *mark), gain, enc_w1, enc_w2)
        return (v["part", i],)

    @named("encode_sum")
    def encode_sum(i, mark):
        own = after(v["part", i], *mark)
        if n_tp == 2:
            v["sum", i] = (own, swap(own, "tp", 1))
        else:
            v["sum", i] = (lax.psum(own, "tp"),)
        return v["sum", i]

    @named("decode")
    def decode(mark):
        came = after(hidden_came, *mark)
        if n_tp == 2:
            norm = decode_norm(tp_at == 0, hidden, came, dec_gain, n_seq)
        else:
            wide = came.astype(jnp.float32)
            norm = wide * lax.rsqrt(jnp.mean(wide * wide, axis=-1, keepdims=True) + 1e-06) * dec_gain
            norm = norm.astype(jnp.bfloat16).reshape(tok_rows, n_seq, q_rows)
            norm = jnp.moveaxis(norm, 1, 0)
        v["norm"] = (norm, swap(norm, "seq", 1)) if n_core == 2 else (norm,)
        return (norm,)

    @named("keys_values")
    def keys_values(i, mark):
        terms = tuple(after(t, *mark) for t in v["sum", i])
        encoded, *v["kv", i] = project((parts[i],) + terms, key_weight, value_weight)
        if i == 1:
            v["earlier"] = lax.ppermute(
                encoded[piece_rows - key_rows :], "seq", [(i, i + 1) for i in range(n_seq - 1)]
            )
        return tuple(v["kv", i])

    @named("keys_values_earlier")
    def keys_values_earlier(mark):
        v["kv", 2] = project((after(v["earlier"], *mark),), key_weight, value_weight)[1:]
        return tuple(v["kv", 2])

    @named("query_part")
    def query_part(keys, last, mark):
        at = [
            (((z_at - k) % depth) * n_y + (y_at + j) % n_y) * n_core + (core_at + c) % n_core
            for k, j in keys
            for c in range(n_core)
        ]
        norms = tuple(after(n, *mark) for n in v["norm"])
        v["q"] = add_query(
            jnp.stack(at).astype(jnp.int32),
            norms,
            [q_stream.blocks[key] for key in keys],
            v.get("q"),
            jnp.bfloat16 if last else jnp.float32,
        )
        return (v["q"],)

    @named("attention")
    def attention(mark):
        query = v["q"]
        if n_core == 2:
            query = ordered(core_first, query[:tok_rows], swap(query[tok_rows:], "seq", 1), 1)
        grouped = jnp.pad(query, ((1, M - 1), (0, 0)))
        keys, values = zip(v["kv", 2], v["kv", 0], v["kv", 1])
        attn = attend(grouped, keys, values)[1 : tok_rows + 1]
        position = me * tok_rows + jnp.arange(tok_rows, dtype=jnp.int32)[:, None]
        attn = jnp.where(position >= M - 1, attn, jnp.zeros_like(attn))
        v["attn"] = (attn, swap(attn, "seq", 1)) if n_core == 2 else (attn,)
        return (attn,)

    pairs = depth // 2

    def out_part(keys, away, mark):
        stay = jnp.stack(
            [(((z_at - p) % depth) // pairs == tp_at).astype(jnp.int32) for p, j in keys]
        )
        attns = tuple(after(a, *mark) for a in v["attn"])
        blocks = [((o_stream.blocks[p, j],), (o_stream.blocks[p + pairs, j],)) for p, j in keys]
        made = out_products(1 - stay if away else stay, attns, blocks)
        return (made[0], swap(made[1], "seq", 1)) if n_core == 2 else made

    @named("send")
    def send(keys, mark):
        sent = out_part(keys, True, mark)
        came = swap(jnp.concatenate(sent, axis=0), "tp", 1)
        for i, key in enumerate(keys):
            v[("came",) + key] = [came[c * len(keys) + i] for c in range(n_core)]
        return (came,), tuple(sent)

    @named("keep")
    def keep(keys, mark):
        kept = out_part(keys, False, mark)
        for i, key in enumerate(keys):
            v[("piece",) + key] = [(kept[c][i], v[("came",) + key][c]) for c in range(n_core)]
        return tuple(kept)

    v["mixed"] = jnp.zeros_like(hidden)

    def place(keys):
        for p, j in keys:
            first = (((z_at - p) % pairs) * n_y + (y_at + j) % n_y) * n_core * o_cols
            sums = [
                kept.astype(jnp.float32) + came.astype(jnp.float32) for kept, came in v["piece", p, j]
            ]
            branch = ordered(core_first, *sums, 1) if n_core == 2 else sums[0]
            here = lax.dynamic_slice(hidden, (0, first), branch.shape).astype(jnp.float32)
            v["mixed"] = lax.dynamic_update_slice(
                v["mixed"], (here + branch).astype(jnp.bfloat16), (0, first)
            )

    scatters = n_tp == 2 and depth % 4 == 0
    q, o = q_stream, o_stream
    if depth == 4 and n_y == 2:
        plan = [
            [(q, 1, 0, "on"), (q, 0, 1, "y"), (q, 3, 0, "back"), (o, 0, 1, "y")],
            [(q, 2, 0, "on"), (q, 1, 1, "y"), (o, 1, 0, "on"), (q, 3, 1, "y")],
            [(o, 2, 0, "on"), (q, 2, 1, "y")],
            [(o, 3, 0, "back"), (o, 2, 1, "y")],
            [(o, 3, 1, "back"), (o, 1, 1, "y")],
        ]
    else:
        plan = []
        for k in range(1, depth + 1):
            plan.append([(s, k, 0, "on") for s in (q, o) if k < depth])
            plan[-1] += [(s, k - 1, 1, "y") for s in (q, o) if n_y == 2]
        plan.append([])
    last_query = 1 + max(i for i, moves in enumerate(plan) if any(m[0] is q for m in moves))
    arrived = [(q, 0, 0), (o, 0, 0)]
    asked, made = set(), set()
    token = after(jnp.float32(0), q.blocks[0, 0])
    for phase, moves in enumerate(plan):
        mark = (token,) if phase else ()
        for s, k, j, way in moves:
            s.fetch(k, j, way, mark)
        mark = (token,)
        values = ()
        if phase == 0:
            values += encode(0, mark) + encode_sum(0, mark) + encode(1, mark) + (hidden_came,)
        elif phase == 1:
            values += decode(mark) + keys_values(0, mark) + encode_sum(1, v["norm"])
        elif phase == 2:
            values += keys_values(1, mark)
        elif phase == 3:
            values += keys_values_earlier(mark)
        if 1 <= phase <= last_query:
            keys = [(k, j) for s, k, j in arrived if s is q and (k, j) not in asked]
            asked.update(keys)
            values += query_part(keys, phase == last_query, mark)
        if phase == last_query:
            values += attention(mark)
        if phase > last_query and scatters:
            keys = [(p, j) for p in range(pairs) for j in range(n_y)]
            keys = [
                key
                for key in keys
                if key not in made and {(o,) + key, (o, key[0] + pairs, key[1])} <= set(arrived)
            ]
            first = ()
            for j in range(n_y):
                here = [key for key in keys if key[1] == j]
                if here:
                    made.update(here)
                    came, _ = send(here, mark)
                    values += came
                    first = first or came
            if keys:
                keep(keys, first)
        arrived += [m[:3] for m in moves]
        token = after(token, *(s.blocks[k, j] for s, k, j, _ in moves), *values)

    if scatters:
        order = [(p, j) for p in range(pairs) for j in range(n_y)]
        rest = [key for key in order if key not in made]
        sent = send(rest, (token,))[1] if rest else ()
        waiting = [key for key in order if key not in rest and ("piece",) + key not in v]
        if waiting:
            keep(waiting, (token,) + sent)
        place([key for key in order if key not in rest])
        if rest:
            keep(rest, sent)
            place(rest)
        return v["mixed"]

    made = []
    attn = jnp.concatenate(v["attn"], axis=0)
    for k in range(depth):
        for j in range(n_y):
            total = jnp.dot(attn, o_stream.blocks[k, j], preferred_element_type=jnp.float32)
            made.append(total.astype(jnp.bfloat16))
    made = jnp.stack(made, axis=0)[:, None]
    if n_core == 2:
        theirs = swap(made[:, :, tok_rows:], "seq", 1)
        made = jnp.concatenate([made[:, :, :tok_rows], theirs], axis=1)
    made = made.reshape(n_seq, tok_rows, o_cols)
    block = jnp.arange(n_seq, dtype=jnp.int32)
    b_z, b_y, b_c = block // (n_y * n_core), (block // n_core) % n_y, block % n_core
    at = (((z_at - b_z) % depth) * n_y + (b_y - y_at) % n_y) * n_core + (b_c - core_at) % n_core
    whole = jnp.moveaxis(jnp.take(made, at, axis=0), 0, 1).reshape(tok_rows, feat * n_tp)
    branch = lax.psum_scatter(whole, "tp", scatter_dimension=1, tiled=True).astype(jnp.float32)
    return (hidden.astype(jnp.float32) + branch).astype(jnp.bfloat16)


def solution(mesh):
    placed = (
        P("seq", "tp"),
        P("seq", None, None),
        P(),
        P(None, "tp"),
        P("tp", None),
        P(None, "tp"),
        P(None, "tp"),
        P(),
        P("seq", "tp"),
        P("tp", "seq"),
    )
    return jax.shard_map(
        per_device, mesh=mesh, in_specs=placed, out_specs=P("seq", "tp"), check_vma=False
    )
```
